32 devices in a mesh: freq: 2 (over y), shot: 4 (over z), surf: 4 (over x, core).
Axes of the slice: x: 2, y: 2, z: 4, core: 2. Of those that a mesh axis runs over, the one named last changes fastest.
Arguments:
- spectra: bfloat16 [256, 2, 64, 128], P(('freq', 'shot', 'surf')), parts along dimension 0, may hold values from -6 to 6
- block_site: int32 [128, 64], P(('shot', 'surf')), may hold values from 0 to 63, as said below
- live_traces: int32 [128, 64], P(('shot', 'surf')), may hold values from 64 to 128
- taper_class: int32 [128, 64], P(('shot', 'surf')), may hold values from 0 to 7
- taper_table: float32 [8, 128], replicated, may hold values from 0.2 to 1
- operator: bfloat16 [4, 8192, 2048], P('freq', 'shot', 'surf'), parts along dimension 0, may hold values from -0.0625 to 0.0625
Outputs:
- multiples: float32 [256, 2, 2048], P(('freq', 'shot'), None, 'surf'), parts along dimension 0
The draws below stay inside these ranges and needn't reach their ends.
There are 2 independent parts, one for each index of `freq`. The reference program is written for one: setup_inputs(seed, part) draws one part's arguments, and reference() takes and returns one part's arrays. A program takes and returns all parts, laid end to end along the dimension named above; an argument that names none is the same for every part. Nothing has to cross between parts.
Inputs may be any that keep to these rules, and one draw needn't show every extreme that they name: `block_site`: the 64 entries of a shot are distinct surface blocks, 16 in each of 4 surface groups (group = block // 16). All 8 consecutive shots that one device holds, at index i along shot, record in the same groups (i + j + k) mod 4, k from 0 to 3, with one j of 0 to 0 for the device. So every device has exactly 128 blocks in each of its 4 groups.
All inputs are finite; a program needn't handle non-finite values.
Results may differ from the reference program's by a relative error of at most 0.0029.
Values may be sent and summed in bfloat16 or wider, within the bound.
A program may use at most 128 MiB of HBM per device.

```python
import jax
import jax.numpy as jnp
from jax import lax

TRACES = 128
BLK_SHOT = 64
GROUP_BLK = 16
SHOT_LOC = 8
TAPERS = 8
SHOTS = 128
SURFACE = 8192
RECV = 2048
N_SHOT = 4
N_SURF = 4


def draw_block_site(key, part):
    key = jax.random.fold_in(key, 11)
    window = min(8, N_SHOT)
    stride = N_SHOT // window
    jitter = min(max(window // 4, 1), stride)
    per_group = BLK_SHOT // window
    devices = SHOTS // SHOT_LOC
    key_device = jax.random.fold_in(key, 2)
    key_pick = jax.random.fold_in(key, 4)
    device_index = jnp.arange(devices, dtype=jnp.int32)
    shot_index = device_index // N_SURF
    surf_index = device_index % N_SURF
    random_start = jax.random.randint(key_device, (devices,), 0, jitter).astype(jnp.int32)
    device_start = jnp.where(surf_index == 0, shot_index % jitter, random_start)
    window_start = jnp.repeat(shot_index + device_start, SHOT_LOC)
    groups = (window_start[:, None] + jnp.arange(window, dtype=jnp.int32)[None, :] * stride) % N_SHOT
    scores = jax.random.randint(key_pick, (SHOTS, window, GROUP_BLK), 0, 2 ** 20)
    scores = scores * GROUP_BLK + jnp.arange(GROUP_BLK, dtype=jnp.int32)[None, None, :]
    chosen = jnp.argsort(scores, axis=-1, stable=True)[:, :, :per_group].astype(jnp.int32)
    return (groups[:, :, None] * GROUP_BLK + chosen).reshape(SHOTS, BLK_SHOT).astype(jnp.int32)


def place_ends(drawn, own_key, least, largest):
    longest = drawn.shape.index(max(drawn.shape))
    spots = []
    for shift in (0, 1):
        where = [jax.random.randint(jax.random.fold_in(own_key, axis), (), 0, length) for axis, length in enumerate(drawn.shape)]
        where[longest] = (where[longest] + shift) % drawn.shape[longest]
        spots.append(tuple(where))
    return drawn.at[spots[0]].set(least).at[spots[1]].set(largest)


def steps_of(stream_key, extent, cuts, low, top_value):
    factor_of, own = 1.0, jax.random.fold_in(stream_key, 6)
    for position, shards_of in cuts:
        heights = jnp.exp(jax.random.uniform(jax.random.fold_in(own, position), (shards_of,), jnp.float32, low / len(cuts), top_value / len(cuts)))
        factor_of = factor_of * jnp.repeat(heights, extent[position] // shards_of).reshape([-1 if axis == position else 1 for axis in range(len(extent))])
    return factor_of


def normal_values(key, dims, width, bound, split=(), held_as=jnp.bfloat16):
    level = steps_of(key, dims, split, -0.22, 0.18) if split else 1.0
    drawn = jax.random.normal(key, dims, jnp.float32) * width * level
    return jnp.minimum(jnp.maximum(drawn, -bound), bound).astype(held_as)


def setup_inputs(seed: int = 0, part: int = 0) -> dict:
    key_list = jax.random.split(jax.random.key(seed), 7)
    part_splits = jax.random.split(jax.random.fold_in(key_list[6], part), 7)
    spectra = normal_values(part_splits[0], (SHOTS, 2, BLK_SHOT, TRACES), 1.0, 6.0, ((0, 16),))
    block_site = draw_block_site(jax.random.fold_in(key_list[6], 71), part)
    live_traces = place_ends(jax.random.randint(key_list[2], (SHOTS, BLK_SHOT), TRACES // 2, TRACES + 1), jax.random.fold_in(key_list[2], 1), TRACES // 2, TRACES).astype(jnp.int32)
    taper_class = place_ends(jax.random.randint(key_list[3], (SHOTS, BLK_SHOT), 0, TAPERS), jax.random.fold_in(key_list[3], 1), 0, TAPERS - 1).astype(jnp.int32)
    taper_table = jnp.clip(jax.random.uniform(key_list[4], (TAPERS, TRACES), jnp.float32, 0.2, 1.0), 0.2, 1.0)
    operator = normal_values(part_splits[5], (2, SURFACE, RECV), (BLK_SHOT * TRACES) ** -0.5, 0.0625, ((1, 4), (2, 4)))
    return dict(spectra=spectra, block_site=block_site, live_traces=live_traces, taper_class=taper_class, taper_table=taper_table, operator=operator)


def reference(spectra, block_site, live_traces, taper_class, taper_table, operator):
    trace_lane = jnp.arange(TRACES, dtype=jnp.int32)
    live_mask = trace_lane[None, None, :] < live_traces[:, :, None]
    weights = jnp.where(live_mask, taper_table[taper_class], 0.0).astype(jnp.float32)
    tapered = (spectra.astype(jnp.float32) * weights[:, None]).astype(jnp.bfloat16)

    def one_shot(shot_args):
        shot_data, shot_sites = shot_args
        row_index = (shot_sites[:, None] * TRACES + trace_lane[None, :]).reshape(-1).astype(jnp.int32)
        gathered = jnp.take(operator, row_index, axis=1)
        flat_data = shot_data.reshape(2, -1)
        real_part = jnp.dot(flat_data[0], gathered[0], preferred_element_type=jnp.float32) - jnp.dot(flat_data[1], gathered[1], preferred_element_type=jnp.float32)
        imag_part = jnp.dot(flat_data[0], gathered[1], preferred_element_type=jnp.float32) + jnp.dot(flat_data[1], gathered[0], preferred_element_type=jnp.float32)
        return jnp.stack([real_part, imag_part])

    return lax.map(one_shot, (tapered, block_site))
```

```python
import functools

import jax
import jax.numpy as jnp
from jax import lax
from jax.experimental import pallas as pl
from jax.experimental.pallas import tpu as pltpu
from jax.sharding import PartitionSpec as P

MESH = pl.DeviceIdType.MESH
PIECES = 1


def flip(index, bits, size):
    total, unit = 0, 1
    while unit < size:
        total = total + unit * (((index // unit) % 2 + (bits // unit) % 2) % 2)
        unit *= 2
    return total


def kernel(
    groups, columns,
    spectra_hbm, site_hbm, live_hbm, class_hbm, table_hbm, operator_hbm, out_ref,
    spectra, site, live, classes, table, operator,
    outgoing, data, near_out, near_in, far_out, far_in,
    load_sem, z_send, z_recv, x_send, x_recv, c_send, c_recv, near_send, near_recv, far_send, far_recv,
):
    me = lax.axis_index("shot")
    column = lax.axis_index("surf")
    across = flip(column, 2, columns)
    beside = flip(column, 1, columns)
    neighbour = flip(me, 1, groups)
    shots, _, blocks, traces = spectra.shape
    tapers = table.shape[0]
    group_blocks = operator.shape[1] // traces
    piece_blocks = group_blocks // PIECES
    depth = piece_blocks * traces
    receivers = operator.shape[2]

    def load(source, target, slot):
        return pltpu.make_async_copy(source, target, load_sem.at[slot])

    small = [
        load(spectra_hbm, spectra, 0),
        load(site_hbm, site, 1),
        load(live_hbm, live, 2),
        load(class_hbm, classes, 3),
        load(table_hbm, table, 4),
    ]
    large = load(operator_hbm, operator, 5)
    for copy in small:
        copy.start()
    large.start()

    barrier = pltpu.get_barrier_semaphore()
    for k in range(1, groups):
        pl.semaphore_signal(barrier, inc=1, device_id={"shot": flip(me, k, groups)}, device_id_type=MESH)
    for partner in (across, beside):
        pl.semaphore_signal(barrier, inc=1, device_id={"surf": partner}, device_id_type=MESH)

    for copy in small:
        copy.wait()

    lane = lax.broadcasted_iota(jnp.int32, (shots, shots * blocks), 1)
    row = lax.broadcasted_iota(jnp.int32, (shots, shots * blocks), 0)
    own = lane // blocks == row
    sites = jnp.where(own, jnp.concatenate([site[...]] * shots, axis=1), -1)
    codes = (classes[...] * 256 + live[...]).astype(jnp.float32)
    codes = jnp.concatenate([codes] * shots, axis=1)
    values = jnp.concatenate(
        [spectra[:, c].reshape(shots * blocks, traces) for c in range(2)], axis=1
    )
    trace_lane = lax.broadcasted_iota(jnp.int32, (group_blocks, shots, traces), 2)

    def place(group):
        point = lax.broadcasted_iota(jnp.int32, (group_blocks, shots, shots * blocks), 0)
        hit = sites[None] == point + group * group_blocks
        pick = jnp.where(hit, 1.0, 0.0).reshape(group_blocks * shots, shots * blocks)
        placed = jnp.dot(pick.astype(jnp.bfloat16), values, preferred_element_type=jnp.float32)
        placed = placed.reshape(group_blocks, shots, 2 * traces)
        code = jnp.sum(jnp.where(hit, codes[None], 0.0), axis=2, keepdims=True).astype(jnp.int32)
        code = jnp.broadcast_to(code, trace_lane.shape)
        taper = code // 256
        weights = jnp.zeros(trace_lane.shape, jnp.float32)
        for k in range(tapers):
            weights = jnp.where(taper == k, table[k : k + 1, :][None], weights)
        weights = jnp.where(trace_lane < code % 256, weights, 0.0)
        return jnp.concatenate(
            [placed[:, :, :traces] * weights, placed[:, :, traces:] * weights], axis=1
        ).astype(jnp.bfloat16)

    def write(placed, target):
        for b in range(group_blocks):
            h, at = b // piece_blocks, (b % piece_blocks) * traces
            target(h)[:, at : at + traces] = placed[b]

    def z_copy(k, h):
        return pltpu.make_async_remote_copy(
            src_ref=outgoing.at[k, h], dst_ref=data.at[me, h, column],
            send_sem=z_send.at[k, h], recv_sem=z_recv.at[k, h],
            device_id={"shot": flip(me, k, groups)}, device_id_type=MESH,
        )

    def z_arrival(k, h):
        other = flip(me, k, groups)
        return pltpu.make_async_remote_copy(
            src_ref=outgoing.at[k, h], dst_ref=data.at[other, h, column],
            send_sem=z_send.at[k, h], recv_sem=z_recv.at[k, h],
            device_id={"shot": other}, device_id_type=MESH,
        )

    def x_copy(k, h, owner):
        slot = data.at[flip(me, k, groups), h, owner]
        return pltpu.make_async_remote_copy(
            src_ref=slot, dst_ref=slot,
            send_sem=x_send.at[k, h], recv_sem=x_recv.at[k, h],
            device_id={"surf": across}, device_id_type=MESH,
        )

    def c_copy(k, h, forwarded, owner):
        slot = data.at[flip(me, k, groups), h, owner]
        return pltpu.make_async_remote_copy(
            src_ref=slot, dst_ref=slot,
            send_sem=c_send.at[k, h, forwarded], recv_sem=c_recv.at[k, h, forwarded],
            device_id={"surf": beside}, device_id_type=MESH,
        )

    def pass_on(k, h):
        x_copy(k, h, column).start()
        c_copy(k, h, 0, column).start()

    def arrive(k, h):
        z_arrival(k, h).wait_recv()
        pass_on(k, h)

    def relay(k, h):
        x_copy(k, h, across).wait_recv()
        c_copy(k, h, 1, across).start()

    def share(k):
        real = imag = 0.0
        for h in range(PIECES):
            c_copy(k, h, 0, beside).wait_recv()
            c_copy(k, h, 1, flip(across, 1, columns)).wait_recv()
            rows = data[flip(me, k, groups), h].reshape(columns * 2 * shots, depth)
            at = h * depth
            real += jnp.dot(rows, operator[0, at : at + depth, :], preferred_element_type=jnp.float32)
            imag += jnp.dot(rows, operator[1, at : at + depth, :], preferred_element_type=jnp.float32)
        real = real.reshape(columns, 2, shots, receivers)
        imag = imag.reshape(columns, 2, shots, receivers)
        return jnp.concatenate(
            [(real[:, 0] - imag[:, 1])[:, None], (imag[:, 0] + real[:, 1])[:, None]], axis=1
        ).reshape(columns * 2 * shots, receivers)

    def near_copy(j):
        return pltpu.make_async_remote_copy(
            src_ref=near_out.at[j], dst_ref=near_in.at[j],
            send_sem=near_send.at[j], recv_sem=near_recv.at[j],
            device_id={"shot": neighbour}, device_id_type=MESH,
        )

    def far_copy(j):
        return pltpu.make_async_remote_copy(
            src_ref=far_out.at[j], dst_ref=far_in.at[j],
            send_sem=far_send.at[j], recv_sem=far_recv.at[j],
            device_id={"shot": flip(me, 2 * j, groups)}, device_id_type=MESH,
        )

    def share_near(j):
        near_out[j] = share(2 * j + 1).astype(jnp.bfloat16)
        near_copy(j).start()

    def share_far(j):
        mine = share(2 * j)
        near_copy(j).wait_recv()
        far_out[j] = (mine + near_in[j].astype(jnp.float32)).astype(jnp.bfloat16)
        far_copy(j).start()

    def share_own():
        out_ref[...] = share(0)

    def send_group(k):
        write(place(flip(me, k, groups)), lambda h: outgoing.at[k, h])
        for h in range(PIECES):
            z_copy(k, h).start()

    pieces = range(PIECES)
    if groups <= 4:
        order = [3, 2, 1][3 - (groups - 1) :]
        first = True
        for k in order:
            write(place(flip(me, k, groups)), lambda h: outgoing.at[k, h])
            if first:
                pl.semaphore_wait(barrier, groups + 1)
                first = False
            for h in pieces:
                z_copy(k, h).start()
        write(place(me), lambda h: data.at[me, h, column])
        for h in pieces:
            pass_on(0, h)
        for h in pieces:
            relay(0, h)
        large.wait()
        share_own()
        if groups == 4:
            for k in (1, 3, 2):
                for h in pieces:
                    arrive(k, h)
                if k == 3:
                    for h in pieces:
                        relay(1, h)
                    share_near(0)
            for h in pieces:
                relay(3, h)
            for h in pieces:
                relay(2, h)
            share_near(1)
            share_far(1)
        else:
            for h in pieces:
                arrive(1, h)
            for h in pieces:
                relay(1, h)
            share_near(0)
    else:
        pl.semaphore_wait(barrier, groups + 1)
        pl.loop(1, groups)(send_group)
        write(place(me), lambda h: data.at[me, h, column])

        for h in pieces:
            pass_on(0, h)

        @pl.loop(1, groups)
        def _(k):
            for h in pieces:
                arrive(k, h)

        @pl.loop(0, groups)
        def _(k):
            for h in pieces:
                relay(k, h)

        large.wait()
        share_own()
        share_near(0)

        @pl.loop(1, groups // 2)
        def _(j):
            share_near(j)
            share_far(j)

    near_copy(0).wait_recv()
    out_ref[...] += near_in[0].astype(jnp.float32)

    def collect(j):
        far_copy(j).wait_recv()
        out_ref[...] += far_in[j].astype(jnp.float32)

    def drain(k):
        for h in pieces:
            x_copy(k, h, column).wait_send()
            c_copy(k, h, 0, column).wait_send()
            c_copy(k, h, 1, across).wait_send()

    def drain_z(k):
        for h in pieces:
            z_copy(k, h).wait_send()

    def repeat(first, last, body):
        if groups <= 4:
            for k in range(first, last):
                body(k)
        else:
            pl.loop(first, last)(body)

    repeat(1, groups // 2, collect)
    repeat(0, groups, drain)
    repeat(1, groups, drain_z)
    repeat(0, groups // 2, lambda j: near_copy(j).wait_send())
    repeat(1, groups // 2, lambda j: far_copy(j).wait_send())


def local(spectra, block_site, live_traces, taper_class, taper_table, operator):
    groups = lax.axis_size("shot")
    columns = lax.axis_size("surf")
    shots, _, _, traces = spectra.shape
    depth = operator.shape[1] // PIECES
    receivers = operator.shape[2]
    rows = columns * 2 * shots
    halves = groups // 2
    dma = pltpu.SemaphoreType.DMA
    result = pl.pallas_call(
        functools.partial(kernel, groups, columns),
        out_shape=jax.ShapeDtypeStruct((rows, receivers), jnp.float32),
        in_specs=[pl.BlockSpec(memory_space=pl.ANY)] * 6,
        out_specs=pl.BlockSpec(memory_space=pltpu.VMEM),
        scratch_shapes=[
            pltpu.VMEM(spectra.shape, spectra.dtype),
            pltpu.VMEM(block_site.shape, jnp.int32),
            pltpu.VMEM(live_traces.shape, jnp.int32),
            pltpu.VMEM(taper_class.shape, jnp.int32),
            pltpu.VMEM(taper_table.shape, jnp.float32),
            pltpu.VMEM(operator.shape, operator.dtype),
            pltpu.VMEM((groups, PIECES, 2 * shots, depth), jnp.bfloat16),
            pltpu.VMEM((groups, PIECES, columns, 2 * shots, depth), jnp.bfloat16),
            pltpu.VMEM((halves, rows, receivers), jnp.bfloat16),
            pltpu.VMEM((halves, rows, receivers), jnp.bfloat16),
            pltpu.VMEM((halves, rows, receivers), jnp.bfloat16),
            pltpu.VMEM((halves, rows, receivers), jnp.bfloat16),
            dma((6,)),
            dma((groups, PIECES)),
            dma((groups, PIECES)),
            dma((groups, PIECES)),
            dma((groups, PIECES)),
            dma((groups, PIECES, 2)),
            dma((groups, PIECES, 2)),
            dma((halves,)),
            dma((halves,)),
            dma((halves,)),
            dma((halves,)),
        ],
        compiler_params=pltpu.CompilerParams(
            collective_id=0, has_side_effects=True, vmem_limit_bytes=48 * 2**20
        ),
    )(spectra, block_site, live_traces, taper_class, taper_table, operator)
    result = result.reshape(columns, 2, shots, receivers)
    return result.transpose(0, 2, 1, 3).reshape(columns * shots, 2, receivers)


def solution(mesh):
    return jax.shard_map(
        local,
        mesh=mesh,
        in_specs=(
            P(("freq", "shot", "surf"), None, None, None),
            P(("shot", "surf"), None),
            P(("shot", "surf"), None),
            P(("shot", "surf"), None),
            P(),
            P("freq", "shot", "surf"),
        ),
        out_specs=P(("freq", "shot"), None, "surf"),
        check_vma=False,
    )
```

```python
import functools

import jax
import jax.numpy as jnp
from jax import lax
from jax.experimental import pallas as pl
from jax.experimental.pallas import tpu as pltpu
from jax.sharding import PartitionSpec as P

MESH = pl.DeviceIdType.MESH
PIECES = 1
SENDS = (1, 0, 2, 3)
STEPS = (
    ("relay", 0, 0),
    ("arrive", 1, 0),
    ("arrive", 2, 0),
    ("multiply", 0, 0),
    ("keep", 0, 0),
    ("relay", 1, 0),
    ("arrive", 3, 0),
    ("relay", 2, 0),
    ("multiply", 1, 0),
    ("send", 1, 0),
    ("relay", 3, 0),
    ("multiply", 2, 0),
    ("send", 2, 0),
    ("multiply", 3, 0),
    ("send", 3, 0),
)


def flip(index, bits, size):
    total, unit = 0, 1
    while unit < size:
        total = total + unit * (((index // unit) % 2 + (bits // unit) % 2) % 2)
        unit *= 2
    return total


def kernel(
    groups, columns,
    spectra_hbm, site_hbm, live_hbm, class_hbm, table_hbm, operator_hbm, own_hbm, incoming_hbm,
    spectra, site, live, classes, table, operator,
    outgoing, data, share_out, own_share,
    load_sem, z_send, z_recv, x_send, x_recv, c_send, c_recv, share_send, share_recv,
):
    me = lax.axis_index("shot")
    column = lax.axis_index("surf")
    across = flip(column, 2, columns)
    beside = flip(column, 1, columns)
    shots, _, blocks, traces = spectra.shape
    tapers = table.shape[0]
    group_blocks = operator.shape[1] // traces
    piece_blocks = group_blocks // PIECES
    depth = piece_blocks * traces
    receivers = operator.shape[2]

    def load(source, target, slot):
        return pltpu.make_async_copy(source, target, load_sem.at[slot])

    small = [
        load(spectra_hbm, spectra, 0),
        load(site_hbm, site, 1),
        load(live_hbm, live, 2),
        load(class_hbm, classes, 3),
        load(table_hbm, table, 4),
    ]
    large = load(operator_hbm, operator, 5)
    for copy in small:
        copy.start()
    large.start()

    barrier = pltpu.get_barrier_semaphore()
    for k in range(1, groups):
        pl.semaphore_signal(barrier, inc=1, device_id={"shot": flip(me, k, groups)}, device_id_type=MESH)
    for partner in (across, beside):
        pl.semaphore_signal(barrier, inc=1, device_id={"surf": partner}, device_id_type=MESH)

    for copy in small:
        copy.wait()

    lane = lax.broadcasted_iota(jnp.int32, (shots, shots * blocks), 1)
    row = lax.broadcasted_iota(jnp.int32, (shots, shots * blocks), 0)
    own = lane // blocks == row
    sites = jnp.where(own, jnp.concatenate([site[...]] * shots, axis=1), -1)
    codes = (classes[...] * 256 + live[...]).astype(jnp.float32)
    codes = jnp.concatenate([codes] * shots, axis=1)
    values = jnp.concatenate(
        [spectra[:, c].reshape(shots * blocks, traces) for c in range(2)], axis=1
    )
    trace_lane = lax.broadcasted_iota(jnp.int32, (group_blocks, shots, traces), 2)

    def place(group):
        point = lax.broadcasted_iota(jnp.int32, (group_blocks, shots, shots * blocks), 0)
        hit = sites[None] == point + group * group_blocks
        pick = jnp.where(hit, 1.0, 0.0).reshape(group_blocks * shots, shots * blocks)
        placed = jnp.dot(pick.astype(jnp.bfloat16), values, preferred_element_type=jnp.float32)
        placed = placed.reshape(group_blocks, shots, 2 * traces)
        code = jnp.sum(jnp.where(hit, codes[None], 0.0), axis=2, keepdims=True).astype(jnp.int32)
        code = jnp.broadcast_to(code, trace_lane.shape)
        taper = code // 256
        weights = jnp.zeros(trace_lane.shape, jnp.float32)
        for k in range(tapers):
            weights = jnp.where(taper == k, table[k : k + 1, :][None], weights)
        weights = jnp.where(trace_lane < code % 256, weights, 0.0)
        return jnp.concatenate(
            [placed[:, :, :traces] * weights, placed[:, :, traces:] * weights], axis=1
        ).astype(jnp.bfloat16)

    def write(placed, target):
        for b in range(group_blocks):
            h, at = b // piece_blocks, (b % piece_blocks) * traces
            target(h)[:, at : at + traces] = placed[b]

    def z_copy(k, h):
        return pltpu.make_async_remote_copy(
            src_ref=outgoing.at[k, h], dst_ref=data.at[me, h, column],
            send_sem=z_send.at[k, h], recv_sem=z_recv.at[k, h],
            device_id={"shot": flip(me, k, groups)}, device_id_type=MESH,
        )

    def z_arrival(k, h):
        other = flip(me, k, groups)
        return pltpu.make_async_remote_copy(
            src_ref=outgoing.at[k, h], dst_ref=data.at[other, h, column],
            send_sem=z_send.at[k, h], recv_sem=z_recv.at[k, h],
            device_id={"shot": other}, device_id_type=MESH,
        )

    def x_copy(k, h, owner):
        slot = data.at[flip(me, k, groups), h, owner]
        return pltpu.make_async_remote_copy(
            src_ref=slot, dst_ref=slot,
            send_sem=x_send.at[k, h], recv_sem=x_recv.at[k, h],
            device_id={"surf": across}, device_id_type=MESH,
        )

    def c_copy(k, h, forwarded, owner):
        slot = data.at[flip(me, k, groups), h, owner]
        return pltpu.make_async_remote_copy(
            src_ref=slot, dst_ref=slot,
            send_sem=c_send.at[k, h, forwarded], recv_sem=c_recv.at[k, h, forwarded],
            device_id={"surf": beside}, device_id_type=MESH,
        )

    def pass_on(k, h):
        x_copy(k, h, column).start()
        c_copy(k, h, 0, column).start()

    def arrive(k, h):
        z_arrival(k, h).wait_recv()
        pass_on(k, h)

    def relay(k, h):
        x_copy(k, h, across).wait_recv()
        c_copy(k, h, 1, across).start()

    def products(k, h):
        c_copy(k, h, 0, beside).wait_recv()
        c_copy(k, h, 1, flip(across, 1, columns)).wait_recv()
        rows = data[flip(me, k, groups), h].reshape(columns * 2 * shots, depth)
        at = h * depth
        return [
            jnp.dot(rows, operator[d, at : at + depth, :], preferred_element_type=jnp.float32)
            for d in range(2)
        ]

    def combine(parts):
        first, second = [
            sum(part[d] for part in parts).reshape(columns, 2, shots, receivers) for d in range(2)
        ]
        return jnp.concatenate(
            [(first[:, 0] - second[:, 1])[:, None], (second[:, 0] + first[:, 1])[:, None]], axis=1
        ).reshape(columns * 2 * shots, receivers)

    def share(k):
        return combine([products(k, h) for h in range(PIECES)])

    def share_copy(k):
        return pltpu.make_async_remote_copy(
            src_ref=share_out.at[k - 1], dst_ref=incoming_hbm.at[k - 1],
            send_sem=share_send.at[k], recv_sem=share_recv.at[k],
            device_id={"shot": flip(me, k, groups)}, device_id_type=MESH,
        )

    def send_share(k, mine):
        share_out[k - 1] = mine.astype(jnp.bfloat16)
        share_copy(k).start()

    def keep_share(mine):
        own_share[...] = mine
        load(own_share, own_hbm, 6).start()

    def send_group(k):
        write(place(flip(me, k, groups)), lambda h: outgoing.at[k, h])
        for h in range(PIECES):
            z_copy(k, h).start()

    pieces = range(PIECES)
    if groups == 4:
        done = {k: [] for k in range(groups)}

        def multiply(k, h):
            done[k].append(products(k, h))

        for position, k in enumerate(SENDS):
            if k == 0:
                write(place(me), lambda h: data.at[me, h, column])
            else:
                write(place(flip(me, k, groups)), lambda h: outgoing.at[k, h])
            if position == 0:
                pl.semaphore_wait(barrier, groups + 1)
            for h in pieces:
                if k == 0:
                    pass_on(0, h)
                else:
                    z_copy(k, h).start()
        for step, k, h in STEPS:
            if step == "arrive":
                arrive(k, h)
            elif step == "relay":
                relay(k, h)
            elif step == "multiply":
                if k == 0 and h == 0:
                    large.wait()
                multiply(k, h)
            elif step == "send":
                send_share(k, combine(done[k]))
            elif step == "keep":
                keep_share(combine(done[k]))
    else:
        pl.semaphore_wait(barrier, groups + 1)
        pl.loop(1, groups)(send_group)
        write(place(me), lambda h: data.at[me, h, column])

        for h in pieces:
            pass_on(0, h)

        @pl.loop(1, groups)
        def _(k):
            for h in pieces:
                arrive(k, h)

        @pl.loop(0, groups)
        def _(k):
            for h in pieces:
                relay(k, h)

        large.wait()
        keep_share(share(0))

        @pl.loop(1, groups)
        def _(k):
            send_share(k, share(k))

    def drain(k):
        for h in pieces:
            x_copy(k, h, column).wait_send()
            c_copy(k, h, 0, column).wait_send()
            c_copy(k, h, 1, across).wait_send()

    def drain_z(k):
        for h in pieces:
            z_copy(k, h).wait_send()

    def repeat(first, last, body):
        if groups <= 4:
            for k in range(first, last):
                body(k)
        else:
            pl.loop(first, last)(body)

    repeat(0, groups, drain)
    repeat(1, groups, drain_z)
    repeat(1, groups, lambda k: share_copy(k).wait())
    load(own_share, own_hbm, 6).wait()


def local(spectra, block_site, live_traces, taper_class, taper_table, operator):
    groups = lax.axis_size("shot")
    columns = lax.axis_size("surf")
    shots, _, _, traces = spectra.shape
    depth = operator.shape[1] // PIECES
    receivers = operator.shape[2]
    rows = columns * 2 * shots
    dma = pltpu.SemaphoreType.DMA
    own, incoming = pl.pallas_call(
        functools.partial(kernel, groups, columns),
        out_shape=(
            jax.ShapeDtypeStruct((rows, receivers), jnp.float32),
            jax.ShapeDtypeStruct((groups - 1, rows, receivers), jnp.bfloat16),
        ),
        in_specs=[pl.BlockSpec(memory_space=pl.ANY)] * 6,
        out_specs=[pl.BlockSpec(memory_space=pl.ANY)] * 2,
        scratch_shapes=[
            pltpu.VMEM(spectra.shape, spectra.dtype),
            pltpu.VMEM(block_site.shape, jnp.int32),
            pltpu.VMEM(live_traces.shape, jnp.int32),
            pltpu.VMEM(taper_class.shape, jnp.int32),
            pltpu.VMEM(taper_table.shape, jnp.float32),
            pltpu.VMEM(operator.shape, operator.dtype),
            pltpu.VMEM((groups, PIECES, 2 * shots, depth), jnp.bfloat16),
            pltpu.VMEM((groups, PIECES, columns, 2 * shots, depth), jnp.bfloat16),
            pltpu.VMEM((groups - 1, rows, receivers), jnp.bfloat16),
            pltpu.VMEM((rows, receivers), jnp.float32),
            dma((7,)),
            dma((groups, PIECES)),
            dma((groups, PIECES)),
            dma((groups, PIECES)),
            dma((groups, PIECES)),
            dma((groups, PIECES, 2)),
            dma((groups, PIECES, 2)),
            dma((groups,)),
            dma((groups,)),
        ],
        compiler_params=pltpu.CompilerParams(
            collective_id=0, has_side_effects=True, vmem_limit_bytes=56 * 2**20
        ),
    )(spectra, block_site, live_traces, taper_class, taper_table, operator)
    total = sum((incoming[k].astype(jnp.float32) for k in range(groups - 1)), own)
    total = total.reshape(columns, 2, shots, receivers)
    return total.transpose(0, 2, 1, 3).reshape(columns * shots, 2, receivers)


def solution(mesh):
    return jax.shard_map(
        local,
        mesh=mesh,
        in_specs=(
            P(("freq", "shot", "surf"), None, None, None),
            P(("shot", "surf"), None),
            P(("shot", "surf"), None),
            P(("shot", "surf"), None),
            P(),
            P("freq", "shot", "surf"),
        ),
        out_specs=P(("freq", "shot"), None, "surf"),
        check_vma=False,
    )
```

```python
import functools

import jax
import jax.numpy as jnp
from jax import lax
from jax.experimental import pallas as pl
from jax.experimental.pallas import tpu as pltpu
from jax.sharding import PartitionSpec as P

MESH = pl.DeviceIdType.MESH
PIECES = 1
SPANS = 1
SENDS = (2, 0, 1, 3)
STEPS = (
    ("relay", 0, 0),
    ("arrive", 2, 0),
    ("arrive", 1, 0),
    ("keep", 0, 0),
    ("relay", 2, 0),
    ("arrive", 3, 0),
    ("relay", 1, 0),
    ("send", 2, 0),
    ("relay", 3, 0),
    ("send", 3, 0),
    ("send", 1, 0),
)


def flip(index, bits, size):
    total, unit = 0, 1
    while unit < size:
        total = total + unit * (((index // unit) % 2 + (bits // unit) % 2) % 2)
        unit *= 2
    return total


def kernel(
    groups, columns,
    spectra_hbm, site_hbm, live_hbm, class_hbm, table_hbm, operator_hbm, own_hbm, incoming_hbm,
    spectra, site, live, classes, table, operator,
    outgoing, data, share_out, own_share,
    load_sem, z_send, z_recv, x_send, x_recv, c_send, c_recv, share_send, share_recv,
):
    me = lax.axis_index("shot")
    column = lax.axis_index("surf")
    across = flip(column, 2, columns)
    beside = flip(column, 1, columns)
    shots, _, blocks, traces = spectra.shape
    tapers = table.shape[0]
    group_blocks = operator.shape[1] // traces
    piece_blocks = group_blocks // PIECES
    depth = piece_blocks * traces
    receivers = operator.shape[2]

    def load(source, target, slot):
        return pltpu.make_async_copy(source, target, load_sem.at[slot])

    small = [
        load(spectra_hbm, spectra, 0),
        load(site_hbm, site, 1),
        load(live_hbm, live, 2),
        load(class_hbm, classes, 3),
        load(table_hbm, table, 4),
    ]
    large = load(operator_hbm, operator, 5)
    for copy in small:
        copy.start()
    large.start()

    barrier = pltpu.get_barrier_semaphore()
    for k in range(1, groups):
        pl.semaphore_signal(barrier, inc=1, device_id={"shot": flip(me, k, groups)}, device_id_type=MESH)
    for partner in (across, beside):
        pl.semaphore_signal(barrier, inc=1, device_id={"surf": partner}, device_id_type=MESH)

    for copy in small:
        copy.wait()

    lane = lax.broadcasted_iota(jnp.int32, (shots, shots * blocks), 1)
    row = lax.broadcasted_iota(jnp.int32, (shots, shots * blocks), 0)
    own = lane // blocks == row
    sites = jnp.where(own, jnp.concatenate([site[...]] * shots, axis=1), -1)
    codes = (classes[...] * 256 + live[...]).astype(jnp.float32)
    codes = jnp.concatenate([codes] * shots, axis=1)
    values = jnp.concatenate(
        [spectra[:, c].reshape(shots * blocks, traces) for c in range(2)], axis=1
    )
    trace_lane = lax.broadcasted_iota(jnp.int32, (group_blocks, shots, traces), 2)

    def place(group):
        point = lax.broadcasted_iota(jnp.int32, (group_blocks, shots, shots * blocks), 0)
        hit = sites[None] == point + group * group_blocks
        pick = jnp.where(hit, 1.0, 0.0).reshape(group_blocks * shots, shots * blocks)
        placed = jnp.dot(pick.astype(jnp.bfloat16), values, preferred_element_type=jnp.float32)
        placed = placed.reshape(group_blocks, shots, 2 * traces)
        code = jnp.sum(jnp.where(hit, codes[None], 0.0), axis=2, keepdims=True).astype(jnp.int32)
        code = jnp.broadcast_to(code, trace_lane.shape)
        taper = code // 256
        weights = jnp.zeros(trace_lane.shape, jnp.float32)
        for k in range(tapers):
            weights = jnp.where(taper == k, table[k : k + 1, :][None], weights)
        weights = jnp.where(trace_lane < code % 256, weights, 0.0)
        return jnp.concatenate(
            [placed[:, :, :traces] * weights, placed[:, :, traces:] * weights], axis=1
        ).astype(jnp.bfloat16)

    def write(placed, target):
        for b in range(group_blocks):
            h, at = b // piece_blocks, (b % piece_blocks) * traces
            target(h)[:, at : at + traces] = placed[b]

    def z_copy(k, h):
        return pltpu.make_async_remote_copy(
            src_ref=outgoing.at[k, h], dst_ref=data.at[me, h, column],
            send_sem=z_send.at[k, h], recv_sem=z_recv.at[k, h],
            device_id={"shot": flip(me, k, groups)}, device_id_type=MESH,
        )

    def z_arrival(k, h):
        other = flip(me, k, groups)
        return pltpu.make_async_remote_copy(
            src_ref=outgoing.at[k, h], dst_ref=data.at[other, h, column],
            send_sem=z_send.at[k, h], recv_sem=z_recv.at[k, h],
            device_id={"shot": other}, device_id_type=MESH,
        )

    def x_copy(k, h, owner):
        slot = data.at[flip(me, k, groups), h, owner]
        return pltpu.make_async_remote_copy(
            src_ref=slot, dst_ref=slot,
            send_sem=x_send.at[k, h], recv_sem=x_recv.at[k, h],
            device_id={"surf": across}, device_id_type=MESH,
        )

    def c_copy(k, h, forwarded, owner):
        slot = data.at[flip(me, k, groups), h, owner]
        return pltpu.make_async_remote_copy(
            src_ref=slot, dst_ref=slot,
            send_sem=c_send.at[k, h, forwarded], recv_sem=c_recv.at[k, h, forwarded],
            device_id={"surf": beside}, device_id_type=MESH,
        )

    def pass_on(k, h):
        x_copy(k, h, column).start()
        c_copy(k, h, 0, column).start()

    def arrive(k, h):
        z_arrival(k, h).wait_recv()
        pass_on(k, h)

    def relay(k, h):
        x_copy(k, h, across).wait_recv()
        c_copy(k, h, 1, across).start()

    def gathered(k):
        for h in range(PIECES):
            c_copy(k, h, 0, beside).wait_recv()
            c_copy(k, h, 1, flip(across, 1, columns)).wait_recv()

    def share(k, start, width):
        first = second = 0.0
        for h in range(PIECES):
            rows = data[flip(me, k, groups), h].reshape(columns * 2 * shots, depth)
            steps, some = slice(h * depth, (h + 1) * depth), slice(start, start + width)
            first += jnp.dot(rows, operator[0, steps, some], preferred_element_type=jnp.float32)
            second += jnp.dot(rows, operator[1, steps, some], preferred_element_type=jnp.float32)
        first = first.reshape(columns, 2, shots, width)
        second = second.reshape(columns, 2, shots, width)
        return jnp.concatenate(
            [(first[:, 0] - second[:, 1])[:, None], (second[:, 0] + first[:, 1])[:, None]], axis=1
        ).reshape(columns * 2 * shots, width)

    def finish(k):
        gathered(k)
        for part in range(SPANS):
            send_share(k, part, share(k, part * span, span))

    span = receivers // SPANS

    def share_copy(k, part):
        window = (k - 1, slice(None), pl.ds(part * span, span))
        return pltpu.make_async_remote_copy(
            src_ref=share_out.at[window], dst_ref=incoming_hbm.at[window],
            send_sem=share_send.at[k, part], recv_sem=share_recv.at[k, part],
            device_id={"shot": flip(me, k, groups)}, device_id_type=MESH,
        )

    def send_share(k, part, mine):
        share_out[k - 1, :, part * span : (part + 1) * span] = mine.astype(jnp.bfloat16)
        share_copy(k, part).start()

    def keep_share(mine):
        own_share[...] = mine
        load(own_share, own_hbm, 6).start()

    def send_group(k):
        write(place(flip(me, k, groups)), lambda h: outgoing.at[k, h])
        for h in range(PIECES):
            z_copy(k, h).start()

    pieces = range(PIECES)
    if groups == 4:
        for position, k in enumerate(SENDS):
            if k == 0:
                write(place(me), lambda h: data.at[me, h, column])
            else:
                write(place(flip(me, k, groups)), lambda h: outgoing.at[k, h])
            if position == 0:
                pl.semaphore_wait(barrier, groups + 1)
            for h in pieces:
                if k == 0:
                    pass_on(0, h)
                else:
                    z_copy(k, h).start()
        for step, k, h in STEPS:
            if step == "arrive":
                arrive(k, h)
            elif step == "relay":
                relay(k, h)
            elif step == "keep":
                large.wait()
                gathered(0)
                keep_share(share(0, 0, receivers))
            elif step == "send":
                finish(k)
    else:
        pl.semaphore_wait(barrier, groups + 1)
        pl.loop(1, groups)(send_group)
        write(place(me), lambda h: data.at[me, h, column])

        for h in pieces:
            pass_on(0, h)

        @pl.loop(1, groups)
        def _(k):
            for h in pieces:
                arrive(k, h)

        @pl.loop(0, groups)
        def _(k):
            for h in pieces:
                relay(k, h)

        large.wait()
        gathered(0)
        keep_share(share(0, 0, receivers))
        pl.loop(1, groups)(finish)

    def drain(k):
        for h in pieces:
            x_copy(k, h, column).wait_send()
            c_copy(k, h, 0, column).wait_send()
            c_copy(k, h, 1, across).wait_send()

    def drain_z(k):
        for h in pieces:
            z_copy(k, h).wait_send()

    def repeat(first, last, body):
        if groups <= 4:
            for k in range(first, last):
                body(k)
        else:
            pl.loop(first, last)(body)

    repeat(0, groups, drain)
    repeat(1, groups, drain_z)
    for part in range(SPANS):
        repeat(1, groups, lambda k: share_copy(k, part).wait())
    load(own_share, own_hbm, 6).wait()


def local(spectra, block_site, live_traces, taper_class, taper_table, operator):
    groups = lax.axis_size("shot")
    columns = lax.axis_size("surf")
    shots, _, _, traces = spectra.shape
    depth = operator.shape[1] // PIECES
    receivers = operator.shape[2]
    rows = columns * 2 * shots
    dma = pltpu.SemaphoreType.DMA
    own, incoming = pl.pallas_call(
        functools.partial(kernel, groups, columns),
        out_shape=(
            jax.ShapeDtypeStruct((rows, receivers), jnp.float32),
            jax.ShapeDtypeStruct((groups - 1, rows, receivers), jnp.bfloat16),
        ),
        in_specs=[pl.BlockSpec(memory_space=pl.ANY)] * 6,
        out_specs=[pl.BlockSpec(memory_space=pl.ANY)] * 2,
        scratch_shapes=[
            pltpu.VMEM(spectra.shape, spectra.dtype),
            pltpu.VMEM(block_site.shape, jnp.int32),
            pltpu.VMEM(live_traces.shape, jnp.int32),
            pltpu.VMEM(taper_class.shape, jnp.int32),
            pltpu.VMEM(taper_table.shape, jnp.float32),
            pltpu.VMEM(operator.shape, operator.dtype),
            pltpu.VMEM((groups, PIECES, 2 * shots, depth), jnp.bfloat16),
            pltpu.VMEM((groups, PIECES, columns, 2 * shots, depth), jnp.bfloat16),
            pltpu.VMEM((groups - 1, rows, receivers), jnp.bfloat16),
            pltpu.VMEM((rows, receivers), jnp.float32),
            dma((7,)),
            dma((groups, PIECES)),
            dma((groups, PIECES)),
            dma((groups, PIECES)),
            dma((groups, PIECES)),
            dma((groups, PIECES, 2)),
            dma((groups, PIECES, 2)),
            dma((groups, SPANS)),
            dma((groups, SPANS)),
        ],
        compiler_params=pltpu.CompilerParams(
            collective_id=0, has_side_effects=True, vmem_limit_bytes=56 * 2**20
        ),
    )(spectra, block_site, live_traces, taper_class, taper_table, operator)
    total = sum((incoming[k].astype(jnp.float32) for k in range(groups - 1)), own)
    total = total.reshape(columns, 2, shots, receivers)
    return total.transpose(0, 2, 1, 3).reshape(columns * shots, 2, receivers)


def solution(mesh):
    return jax.shard_map(
        local,
        mesh=mesh,
        in_specs=(
            P(("freq", "shot", "surf"), None, None, None),
            P(("shot", "surf"), None),
            P(("shot", "surf"), None),
            P(("shot", "surf"), None),
            P(),
            P("freq", "shot", "surf"),
        ),
        out_specs=P(("freq", "shot"), None, "surf"),
        check_vma=False,
    )
```
